32 devices in a mesh: groups: 2 (over y), frame: 4 (over z), space: 4 (over x, core).
Axes of the slice: x: 2, y: 2, z: 4, core: 2. Of those that a mesh axis runs over, the one named last changes fastest.
Arguments:
- queries: float32 [16384, 128], P(('groups', 'frame', 'space')), parts along dimension 0, may hold values from -256 to 256
- keys: float32 [16384, 128], P(('groups', 'frame', 'space')), parts along dimension 0, may hold values from -8 to 8
- values: float32 [16384, 128], P(('groups', 'frame', 'space')), parts along dimension 0, may hold values from -6 to 6
- block_mask: int32 [4, 4], replicated, may hold values from 0 to 1, as said below
- partner_flags: int32 [4, 2, 2], replicated, may hold values 0 or 1
Outputs:
- attended: float32 [16384, 128], P(('groups', 'frame', 'space')), parts along dimension 0
The draws below stay inside these ranges and needn't reach their ends.
There are 2 independent parts, one for each index of `groups`. The reference program is written for one: setup_inputs(seed, part) draws one part's arguments, and reference() takes and returns one part's arrays. A program takes and returns all parts, laid end to end along the dimension named above; an argument that names none is the same for every part. Nothing has to cross between parts.
Inputs may be any that keep to these rules, and one draw needn't show every extreme that they name: block_mask[a, b] = 1 when a = b or |a - b| = 2, and block_mask[a, b] = 0 when |a - b| > 2. `partner_flags`: a partner outside frame groups 0 to 3 is never used, whatever its flag.
All inputs are finite; a program needn't handle non-finite values.
Results may differ from the reference program's by a relative error of at most 0.0003.
Values sent between devices are 32-bit elements; how exact they have to be, the bound alone decides.
A program may use at most 64 MiB of HBM per device.

```python
import math
import jax
import jax.numpy as jnp
from jax import lax

HEAD = 128
TOK_DEV = 512
GROUPS = 4
BLOCKS = 4
LEVELS = 2
GROUP_TOKENS = 2048
TOKENS = 8192


def draw_pair(key):
    base = jax.random.fold_in(key, 41)
    first_key, second_key = jax.random.split(base, 2)
    keys_all = 1.6 * jax.random.truncated_normal(first_key, -5.0, 5.0, (TOKENS, HEAD), jnp.float32)
    query_all = 1.6 * jax.random.truncated_normal(second_key, -5.0, 5.0, (TOKENS, HEAD), jnp.float32)
    return (query_all, keys_all)


def draw_queries(key, part):
    return draw_pair(key)[0]


def draw_keys(key, part):
    return draw_pair(key)[1]


def draw_block_mask(key, part):
    random_bits = jax.random.randint(jax.random.fold_in(key, 11), (BLOCKS, BLOCKS), 0, 2)
    row_ids = lax.broadcasted_iota(jnp.int32, (BLOCKS, BLOCKS), 0)
    column_ids = lax.broadcasted_iota(jnp.int32, (BLOCKS, BLOCKS), 1)
    spread = jnp.abs(row_ids - column_ids)
    reach = BLOCKS // 2
    inner = jnp.where(spread < reach, random_bits, 0)
    return jnp.where((spread == 0) | (spread == reach), 1, inner).astype(jnp.int32)


def touch_ends(values, rng, low, high):
    index_at = [jax.random.randint(jax.random.fold_in(rng, axis), (), 0, length) for axis, length in enumerate(values.shape)]
    main_axis = values.shape.index(max(values.shape))
    next_to = index_at[:main_axis] + [(index_at[main_axis] + 1) % values.shape[main_axis]] + index_at[main_axis + 1:]
    return values.at[tuple(index_at)].set(low).at[tuple(next_to)].set(high)


def level_of(key, shape, pieces, low, top_value):
    def one(axis_at, parts):
        draws = jax.random.uniform(jax.random.fold_in(jax.random.fold_in(key, 6), axis_at), (parts,), jnp.float32, low / len(pieces), top_value / len(pieces))
        return jnp.repeat(jnp.exp(draws), shape[axis_at] // parts).reshape((-1,) + (1,) * (len(shape) - axis_at - 1))

    level = one(*pieces[0])
    for cut in pieces[1:]:
        level = level * one(*cut)
    return level


def gaussian(key, shape, scale, bound, cuts=(), kind=jnp.bfloat16):
    loudness = level_of(key, shape, cuts, -0.22, 0.18) if cuts else 1.0
    values = jax.random.normal(key, shape, jnp.float32) * scale * loudness
    return jnp.minimum(jnp.maximum(values, -bound), bound).astype(kind)


def setup_inputs(seed: int = 0, part: int = 0) -> dict:
    seeds = jax.random.split(jax.random.key(seed), 6)
    part_splits = jax.random.split(jax.random.fold_in(seeds[5], part), 6)
    return {
        "queries": draw_queries(jax.random.fold_in(jax.random.fold_in(seeds[5], part), 71), part),
        "keys": draw_keys(jax.random.fold_in(jax.random.fold_in(seeds[5], part), 71), part),
        "values": gaussian(part_splits[2], (TOKENS, HEAD), 1.0, 6.0, ((0, 16),), jnp.float32),
        "block_mask": draw_block_mask(jax.random.fold_in(seeds[5], 71), part),
        "partner_flags": touch_ends((jax.random.randint(seeds[4], (GROUPS, LEVELS, 2), 0, 4) < 3).astype(jnp.int32), jax.random.fold_in(seeds[4], 1), 0, 1),
    }


masked_score = -1e+30

def reference(queries, keys, values, block_mask, partner_flags):
    score_scale = 1.0 / math.sqrt(HEAD)
    query_blocks = queries.reshape(GROUPS, BLOCKS, TOK_DEV, HEAD)
    key_blocks = keys.reshape(GROUPS, BLOCKS, TOK_DEV, HEAD)
    value_blocks = values.reshape(GROUPS, BLOCKS, TOK_DEV, HEAD)

    def one_block(block_index):
        group_index = block_index // BLOCKS
        space_index = block_index % BLOCKS
        query_rows = query_blocks[group_index, space_index]
        key_parts = [key_blocks[group_index].reshape(GROUP_TOKENS, HEAD)]
        value_parts = [value_blocks[group_index].reshape(GROUP_TOKENS, HEAD)]
        allowed_parts = [jnp.repeat(block_mask[space_index] > 0, TOK_DEV)]
        for level_index in range(LEVELS):
            distance = 2 ** level_index
            for direction in range(2):
                partner = group_index - distance if direction == 0 else group_index + distance
                usable = (partner >= 0) & (partner < GROUPS) & (partner_flags[group_index, level_index, direction] > 0)
                clamped = jnp.clip(partner, 0, GROUPS - 1).astype(jnp.int32)
                key_parts.append(key_blocks[clamped, space_index])
                value_parts.append(value_blocks[clamped, space_index])
                allowed_parts.append(jnp.broadcast_to(usable, (TOK_DEV,)))
        all_keys = jnp.concatenate(key_parts, axis=0)
        all_values = jnp.concatenate(value_parts, axis=0)
        allowed = jnp.concatenate(allowed_parts, axis=0)
        scores = jnp.dot(query_rows, all_keys.T, precision=lax.Precision.HIGHEST, preferred_element_type=jnp.float32) * score_scale
        scores = jnp.where(allowed[None, :], scores, masked_score)
        row_max = lax.optimization_barrier(jnp.max(scores, axis=1, keepdims=True))
        weights = jnp.where(allowed[None, :], jnp.exp(scores - row_max), 0.0)
        row_total = lax.optimization_barrier(jnp.sum(weights, axis=1, keepdims=True))
        weighted = jnp.dot(weights, all_values, precision=lax.Precision.HIGHEST, preferred_element_type=jnp.float32)
        return weighted / row_total
    result = lax.map(one_block, jnp.arange(GROUPS * BLOCKS, dtype=jnp.int32))
    return result.reshape(TOKENS, HEAD)
```

```python
import functools
import math

import jax
import jax.numpy as jnp
from jax import lax
from jax.experimental import pallas as pl
from jax.experimental.pallas import tpu as pltpu
from jax.sharding import PartitionSpec as P

masked_score = -1e30
MESH = pl.DeviceIdType.MESH


def pieces_of(block, count):
    pieces = []
    rest = block
    for index in range(count):
        piece = rest.astype(jnp.bfloat16)
        pieces.append(piece)
        if index + 1 < count:
            rest = rest - piece.astype(jnp.float32)
    return pieces


def kernel(
    blocks,
    groups,
    levels,
    chunks,
    q_hbm,
    k_hbm,
    v_hbm,
    mask_ref,
    flags_ref,
    out_ref,
    q_vmem,
    space_buf,
    frame_buf,
    query_parts,
    row_max,
    row_total,
    weighted,
    local_sem,
    space_send,
    space_recv,
    frame_send,
    frame_recv,
):
    rows, width = q_vmem.shape
    chunk_rows = rows // chunks
    depth = 2 ** (levels - 1)
    reach = blocks // 2
    chips = blocks // 2
    here = lax.axis_index("space")
    group = lax.axis_index("frame")

    partners = []
    for step in range(1, blocks):
        chip = lax.rem(here // 2 + step // 2, chips)
        core = lax.rem(here % 2 + step % 2, 2)
        other = chip * 2 + core
        distance = jnp.where(other > here, other - here, here - other)
        partners.append((other, distance <= reach))
    routes = [
        (0, group + 1, group + 1 < groups),
        (1, group - 1, group >= 1),
    ]

    local = [
        pltpu.make_async_copy(q_hbm, q_vmem, local_sem.at[0]),
        pltpu.make_async_copy(k_hbm, space_buf.at[here, 0], local_sem.at[1]),
        pltpu.make_async_copy(v_hbm, space_buf.at[here, 1], local_sem.at[2]),
    ]
    for copy in local:
        copy.start()

    barrier = pltpu.get_barrier_semaphore()
    expected = jnp.int32(0)
    for _, target, exists in routes:
        expected = expected + jnp.where(exists, 1, 0)

        @pl.when(exists)
        def _(target=target):
            pl.semaphore_signal(barrier, inc=1, device_id={"frame": target}, device_id_type=MESH)

    for other, near in partners:
        expected = expected + jnp.where(near, 1, 0)

        @pl.when(near)
        def _(other=other):
            pl.semaphore_signal(barrier, inc=1, device_id={"space": other}, device_id_type=MESH)

    pl.semaphore_wait(barrier, expected)

    def frame_copy(way, hop, chunk, part, target):
        span = pl.ds(chunk * chunk_rows, chunk_rows)
        if hop == 1:
            source = (k_hbm, v_hbm)[part].at[span]
        else:
            source = frame_buf.at[way, hop - 2, part, span]
        return pltpu.make_async_remote_copy(
            src_ref=source,
            dst_ref=frame_buf.at[way, hop - 1, part, span],
            send_sem=frame_send.at[way, hop - 1, chunk, part],
            recv_sem=frame_recv.at[way, hop - 1, chunk, part],
            device_id={"frame": target},
            device_id_type=MESH,
        )

    def space_copy(step, part, slot, target):
        return pltpu.make_async_remote_copy(
            src_ref=(k_hbm, v_hbm)[part],
            dst_ref=space_buf.at[slot, part],
            send_sem=space_send.at[step, part],
            recv_sem=space_recv.at[slot, part],
            device_id={"space": target},
            device_id_type=MESH,
        )

    for chunk in range(chunks):
        for way, target, exists in routes:

            @pl.when(exists)
            def _(way=way, target=target, chunk=chunk):
                for part in range(2):
                    frame_copy(way, 1, chunk, part, target).start()

    for step, (other, near) in enumerate(partners):

        @pl.when(near)
        def _(step=step, other=other):
            for part in range(2):
                space_copy(step, part, here, other).start()

    for copy in local:
        copy.wait()

    scale = math.log2(math.e) / math.sqrt(width)
    first, second, third = pieces_of(q_vmem[...] * scale, 3)
    query_parts[...] = jnp.concatenate([first, second, second, first, third, first], axis=1)
    row_max[...] = jnp.full_like(row_max, masked_score)
    row_total[...] = jnp.zeros_like(row_total)
    weighted[...] = jnp.zeros_like(weighted)

    def absorb(key_rows, value_rows, shift):
        k0, k1, k2 = pieces_of(key_rows, 3)
        scores = lax.dot_general(
            jnp.concatenate([k0, k1, k0, k1, k0, k2], axis=1),
            query_parts[...],
            (((1,), (1,)), ((), ())),
            preferred_element_type=jnp.float32,
        )
        old_max = row_max[...]
        new_max = jnp.maximum(old_max, jnp.max(scores, axis=0, keepdims=True) + shift)
        weights = jnp.exp2(scores - (new_max - shift))
        factor = jnp.exp2(old_max - new_max)
        row_max[...] = new_max
        row_total[...] = row_total[...] * factor + jnp.sum(weights, axis=0, keepdims=True)
        v_parts = jnp.concatenate(pieces_of(value_rows, 2), axis=1)
        w0, w1 = pieces_of(weights, 2)
        contract = (((0,), (0,)), ((), ()))
        product = lax.dot_general(v_parts, w0, contract, preferred_element_type=jnp.float32)
        product += lax.dot_general(v_parts, w1, contract, preferred_element_type=jnp.float32)
        weighted[...] = weighted[...] * factor + (product[:width] + product[width:])

    def absorb_space(slot, allowed):
        absorb(space_buf[slot, 0], space_buf[slot, 1], jnp.where(allowed > 0, 0.0, masked_score))

    def take_space(step):
        other, near = partners[step]

        @pl.when(near)
        def _():
            for part in range(2):
                space_copy(step, part, other, other).wait_recv()
            absorb_space(other, mask_ref[here, other])

    def take_frame(hop):
        for chunk in range(chunks):
            for way, target, exists in routes:
                arrives = (group >= hop) if way == 0 else (group + hop < groups)

                @pl.when(arrives)
                def _(way=way, chunk=chunk, target=target):
                    for part in range(2):
                        frame_copy(way, hop, chunk, part, target).wait_recv()

                if hop < depth:

                    @pl.when(arrives & exists)
                    def _(way=way, chunk=chunk, target=target):
                        for part in range(2):
                            frame_copy(way, hop + 1, chunk, part, target).start()

            if hop & (hop - 1):
                continue
            for way, _, _ in routes:
                arrives = (group >= hop) if way == 0 else (group + hop < groups)

                @pl.when(arrives)
                def _(way=way, chunk=chunk):
                    allowed = flags_ref[group, hop.bit_length() - 1, way]
                    span = pl.ds(chunk * chunk_rows, chunk_rows)
                    absorb(
                        frame_buf[way, hop - 1, 0, span],
                        frame_buf[way, hop - 1, 1, span],
                        jnp.where(allowed > 0, 0.0, masked_score),
                    )

    absorb_space(here, mask_ref[here, here])
    take_space(0)
    take_frame(1)
    for step in range(1, blocks - 1):
        take_space(step)
    for hop in range(2, depth + 1):
        take_frame(hop)

    out_ref[...] = (weighted[...] / row_total[...]).T

    for step, (other, near) in enumerate(partners):

        @pl.when(near)
        def _(step=step, other=other):
            for part in range(2):
                space_copy(step, part, here, other).wait_send()

    for hop in range(1, depth + 1):
        for way, target, exists in routes:
            origin = (group >= hop - 1) if way == 0 else (group + hop - 1 < groups)

            @pl.when(exists & origin)
            def _(way=way, hop=hop, target=target):
                for chunk in range(chunks):
                    for part in range(2):
                        frame_copy(way, hop, chunk, part, target).wait_send()


def per_device(queries, keys, values, block_mask, partner_flags):
    rows, width = queries.shape
    blocks = lax.axis_size("space")
    groups = lax.axis_size("frame")
    levels = partner_flags.shape[1]
    depth = 2 ** (levels - 1)
    chunks = 4
    any_space = pl.BlockSpec(memory_space=pl.ANY)
    scalar_space = pl.BlockSpec(memory_space=pltpu.SMEM)
    used = blocks + 2 * levels
    return pl.pallas_call(
        functools.partial(kernel, blocks, groups, levels, chunks),
        out_shape=jax.ShapeDtypeStruct((rows, width), jnp.float32),
        in_specs=[any_space] * 3 + [scalar_space] * 2,
        out_specs=pl.BlockSpec(memory_space=pltpu.VMEM),
        scratch_shapes=[
            pltpu.VMEM((rows, width), jnp.float32),
            pltpu.VMEM((blocks, 2, rows, width), jnp.float32),
            pltpu.VMEM((2, depth, 2, rows, width), jnp.float32),
            pltpu.VMEM((rows, 6 * width), jnp.bfloat16),
            pltpu.VMEM((1, rows), jnp.float32),
            pltpu.VMEM((1, rows), jnp.float32),
            pltpu.VMEM((width, rows), jnp.float32),
            pltpu.SemaphoreType.DMA((3,)),
            pltpu.SemaphoreType.DMA((blocks, 2)),
            pltpu.SemaphoreType.DMA((blocks, 2)),
            pltpu.SemaphoreType.DMA((2, depth, chunks, 2)),
            pltpu.SemaphoreType.DMA((2, depth, chunks, 2)),
        ],
        compiler_params=pltpu.CompilerParams(
            collective_id=0, has_side_effects=True, vmem_limit_bytes=48 * 2**20
        ),
        cost_estimate=pl.CostEstimate(
            flops=4 * used * rows * rows * width,
            bytes_accessed=16 * rows * width,
            transcendentals=used * rows * rows,
        ),
    )(queries, keys, values, block_mask, partner_flags)


def solution(mesh):
    split = P(("groups", "frame", "space"), None)
    return jax.shard_map(
        per_device,
        mesh=mesh,
        in_specs=(split, split, split, P(), P()),
        out_specs=split,
        check_vma=False,
    )
```

```python
import functools
import math

import jax
import jax.numpy as jnp
from jax import lax
from jax.experimental import pallas as pl
from jax.experimental.pallas import tpu as pltpu
from jax.sharding import PartitionSpec as P

masked_score = -1e30
MESH = pl.DeviceIdType.MESH


def pieces_of(block, count):
    pieces = []
    rest = block
    for index in range(count):
        piece = rest.astype(jnp.bfloat16)
        pieces.append(piece)
        if index + 1 < count:
            rest = rest - piece.astype(jnp.float32)
    return pieces


def kernel(
    blocks,
    groups,
    levels,
    chunks,
    q_hbm,
    k_hbm,
    v_hbm,
    mask_hbm,
    flags_hbm,
    out_ref,
    mask_ref,
    flags_ref,
    q_vmem,
    space_buf,
    frame_buf,
    query_parts,
    row_max,
    row_total,
    weighted,
    local_sem,
    space_send,
    space_recv,
    frame_send,
    frame_recv,
):
    rows, width = q_vmem.shape
    chunk_rows = rows // chunks
    depth = 2 ** (levels - 1)
    reach = blocks // 2
    chips = blocks // 2
    here = lax.axis_index("space")
    group = lax.axis_index("frame")

    partners = []
    for step in range(1, blocks):
        chip = lax.rem(here // 2 + step // 2, chips)
        core = lax.rem(here % 2 + step % 2, 2)
        other = chip * 2 + core
        distance = jnp.where(other > here, other - here, here - other)
        partners.append((other, distance <= reach))
    routes = [
        (0, group + 1, group + 1 < groups),
        (1, group - 1, group >= 1),
    ]

    local = [
        pltpu.make_async_copy(q_hbm, q_vmem, local_sem.at[0]),
        pltpu.make_async_copy(k_hbm, space_buf.at[here, 0], local_sem.at[1]),
        pltpu.make_async_copy(v_hbm, space_buf.at[here, 1], local_sem.at[2]),
        pltpu.make_async_copy(mask_hbm, mask_ref, local_sem.at[3]),
        pltpu.make_async_copy(flags_hbm, flags_ref, local_sem.at[4]),
    ]

    barrier = pltpu.get_barrier_semaphore()
    expected = jnp.int32(0)
    for _, target, exists in routes:
        expected = expected + jnp.where(exists, 1, 0)

        @pl.when(exists)
        def _(target=target):
            pl.semaphore_signal(barrier, inc=1, device_id={"frame": target}, device_id_type=MESH)

    for other, near in partners:
        expected = expected + jnp.where(near, 1, 0)

        @pl.when(near)
        def _(other=other):
            pl.semaphore_signal(barrier, inc=1, device_id={"space": other}, device_id_type=MESH)

    for copy in local:
        copy.start()
    pl.semaphore_wait(barrier, expected)

    def frame_copy(way, hop, chunk, part, target):
        span = pl.ds(chunk * chunk_rows, chunk_rows)
        if hop == 1:
            source = (k_hbm, v_hbm)[part].at[span]
        else:
            source = frame_buf.at[way, hop - 2, part, span]
        return pltpu.make_async_remote_copy(
            src_ref=source,
            dst_ref=frame_buf.at[way, hop - 1, part, span],
            send_sem=frame_send.at[way, hop - 1, chunk, part],
            recv_sem=frame_recv.at[way, hop - 1, chunk, part],
            device_id={"frame": target},
            device_id_type=MESH,
        )

    def space_copy(step, part, slot, target):
        return pltpu.make_async_remote_copy(
            src_ref=(k_hbm, v_hbm)[part],
            dst_ref=space_buf.at[slot, part],
            send_sem=space_send.at[step, part],
            recv_sem=space_recv.at[slot, part],
            device_id={"space": target},
            device_id_type=MESH,
        )

    for chunk in range(chunks):
        for way, target, exists in routes:

            @pl.when(exists)
            def _(way=way, target=target, chunk=chunk):
                for part in range(2):
                    frame_copy(way, 1, chunk, part, target).start()

    for step, (other, near) in enumerate(partners):

        @pl.when(near)
        def _(step=step, other=other):
            for part in range(2):
                space_copy(step, part, here, other).start()

    for copy in local:
        copy.wait()

    scale = math.log2(math.e) / math.sqrt(width)
    first, second, third = pieces_of(q_vmem[...] * scale, 3)
    query_parts[...] = jnp.concatenate([first, second, second, first, third, first], axis=1)
    row_max[...] = jnp.full_like(row_max, masked_score)
    row_total[...] = jnp.zeros_like(row_total)
    weighted[...] = jnp.zeros_like(weighted)

    def absorb(key_rows, read_values, shift):
        k0, k1, k2 = pieces_of(key_rows, 3)
        scores = lax.dot_general(
            jnp.concatenate([k0, k1, k0, k1, k0, k2], axis=1),
            query_parts[...],
            (((1,), (1,)), ((), ())),
            preferred_element_type=jnp.float32,
        )
        old_max = row_max[...]
        new_max = jnp.maximum(old_max, jnp.max(scores, axis=0, keepdims=True) + shift)
        weights = jnp.exp2(scores - (new_max - shift))
        factor = jnp.exp2(old_max - new_max)
        row_max[...] = new_max
        row_total[...] = row_total[...] * factor + jnp.sum(weights, axis=0, keepdims=True)
        v_parts = jnp.concatenate(pieces_of(read_values(), 2), axis=1)
        w0, w1 = pieces_of(weights, 2)
        contract = (((0,), (0,)), ((), ()))
        product = lax.dot_general(v_parts, w0, contract, preferred_element_type=jnp.float32)
        product += lax.dot_general(v_parts, w1, contract, preferred_element_type=jnp.float32)
        weighted[...] = weighted[...] * factor + (product[:width] + product[width:])

    def absorb_space(slot, allowed):
        absorb(space_buf[slot, 0], lambda: space_buf[slot, 1], jnp.where(allowed > 0, 0.0, masked_score))

    def take_space(step):
        other, near = partners[step]

        @pl.when(near)
        def _():
            for part in range(2):
                space_copy(step, part, other, other).wait_recv()
            absorb_space(other, mask_ref[here, other])

    def arrives(way, hop):
        return (group >= hop) if way == 0 else (group + hop < groups)

    def take_frame(hop):
        used = hop & (hop - 1) == 0
        passed_on = hop < depth
        lag = min(2, chunks - 1) if hop == 1 else 0

        def pass_on(chunk):
            for way, target, exists in routes:

                @pl.when(arrives(way, hop) & exists)
                def _(way=way, target=target):
                    for part in range(2):
                        frame_copy(way, hop + 1, chunk, part, target).start()

        def attend(way, chunk, before_values):
            allowed = flags_ref[hop.bit_length() - 1, way, group]
            span = pl.ds(chunk * chunk_rows, chunk_rows)

            def read_values():
                before_values()
                return frame_buf[way, hop - 1, 1, span]

            absorb(
                frame_buf[way, hop - 1, 0, span],
                read_values,
                jnp.where(allowed > 0, 0.0, masked_score),
            )

        for chunk in range(chunks):
            for way, target, _ in routes:
                landed = [frame_copy(way, hop, chunk, part, target) for part in range(2)]
                if used and not passed_on:

                    @pl.when(arrives(way, hop))
                    def _(way=way, landed=landed):
                        landed[0].wait_recv()
                        attend(way, chunk, landed[1].wait_recv)

                else:

                    @pl.when(arrives(way, hop))
                    def _(landed=landed):
                        for copy in landed:
                            copy.wait_recv()

            if passed_on and chunk >= lag:
                pass_on(chunk - lag)
                if chunk == chunks - 1:
                    for late in range(chunks - lag, chunks):
                        pass_on(late)
            if used and passed_on:
                for way, _, _ in routes:

                    @pl.when(arrives(way, hop))
                    def _(way=way):
                        attend(way, chunk, lambda: None)

    absorb_space(here, mask_ref[here, here])
    take_space(0)
    take_frame(1)
    for step in range(1, blocks - 1):
        take_space(step)
    for hop in range(2, depth + 1):
        take_frame(hop)

    out_ref[...] = (weighted[...] / row_total[...]).T

    for step, (other, near) in enumerate(partners):

        @pl.when(near)
        def _(step=step, other=other):
            for part in range(2):
                space_copy(step, part, here, other).wait_send()

    for hop in range(1, depth + 1):
        for way, target, exists in routes:

            @pl.when(exists & arrives(way, hop - 1))
            def _(way=way, hop=hop, target=target):
                for chunk in range(chunks):
                    for part in range(2):
                        frame_copy(way, hop, chunk, part, target).wait_send()


def per_device(queries, keys, values, block_mask, partner_flags):
    rows, width = queries.shape
    blocks = lax.axis_size("space")
    groups = lax.axis_size("frame")
    levels = partner_flags.shape[1]
    depth = 2 ** (levels - 1)
    chunks = 4
    used = blocks + 2 * levels
    return pl.pallas_call(
        functools.partial(kernel, blocks, groups, levels, chunks),
        out_shape=jax.ShapeDtypeStruct((rows, width), jnp.float32),
        in_specs=[pl.BlockSpec(memory_space=pltpu.HBM)] * 5,
        out_specs=pl.BlockSpec(memory_space=pltpu.VMEM),
        scratch_shapes=[
            pltpu.SMEM(block_mask.shape, jnp.int32),
            pltpu.SMEM((levels, 2, groups), jnp.int32),
            pltpu.VMEM((rows, width), jnp.float32),
            pltpu.VMEM((blocks, 2, rows, width), jnp.float32),
            pltpu.VMEM((2, depth, 2, rows, width), jnp.float32),
            pltpu.VMEM((rows, 6 * width), jnp.bfloat16),
            pltpu.VMEM((1, rows), jnp.float32),
            pltpu.VMEM((1, rows), jnp.float32),
            pltpu.VMEM((width, rows), jnp.float32),
            pltpu.SemaphoreType.DMA((5,)),
            pltpu.SemaphoreType.DMA((blocks, 2)),
            pltpu.SemaphoreType.DMA((blocks, 2)),
            pltpu.SemaphoreType.DMA((2, depth, chunks, 2)),
            pltpu.SemaphoreType.DMA((2, depth, chunks, 2)),
        ],
        compiler_params=pltpu.CompilerParams(
            collective_id=0, has_side_effects=True, vmem_limit_bytes=48 * 2**20
        ),
        cost_estimate=pl.CostEstimate(
            flops=4 * used * rows * rows * width,
            bytes_accessed=16 * rows * width,
            transcendentals=used * rows * rows,
        ),
    )(queries, keys, values, block_mask, jnp.transpose(partner_flags, (1, 2, 0)))


def solution(mesh):
    split = P(("groups", "frame", "space"), None)
    return jax.shard_map(
        per_device,
        mesh=mesh,
        in_specs=(split, split, split, P(), P()),
        out_specs=split,
        check_vma=False,
    )
```

```python
import functools
import math

import jax
import jax.numpy as jnp
from jax import lax
from jax.experimental import pallas as pl
from jax.experimental.pallas import tpu as pltpu
from jax.sharding import PartitionSpec as P

masked_score = -1e30
MESH = pl.DeviceIdType.MESH


def pieces_of(block, count):
    pieces = []
    rest = block
    for index in range(count):
        piece = rest.astype(jnp.bfloat16)
        pieces.append(piece)
        if index + 1 < count:
            rest = rest - piece.astype(jnp.float32)
    return pieces


def kernel(
    blocks,
    groups,
    levels,
    chunks,
    q_hbm,
    k_hbm,
    v_hbm,
    mask_hbm,
    flags_hbm,
    out_ref,
    mask_ref,
    flags_ref,
    q_vmem,
    space_buf,
    frame_buf,
    query_parts,
    row_max,
    row_total,
    weighted,
    local_sem,
    space_send,
    space_recv,
    frame_send,
    frame_recv,
):
    rows, width = q_vmem.shape
    chunk_rows = rows // chunks
    depth = 2 ** (levels - 1)
    reach = blocks // 2
    chips = blocks // 2
    here = lax.axis_index("space")
    group = lax.axis_index("frame")

    partners = []
    for step in range(1, blocks):
        chip = lax.rem(here // 2 + step // 2, chips)
        core = lax.rem(here % 2 + step % 2, 2)
        other = chip * 2 + core
        distance = jnp.where(other > here, other - here, here - other)
        partners.append((other, distance <= reach))
    routes = [
        (0, group + 1, group + 1 < groups),
        (1, group - 1, group >= 1),
    ]

    local = [
        pltpu.make_async_copy(q_hbm, q_vmem, local_sem.at[0]),
        pltpu.make_async_copy(k_hbm, space_buf.at[here, 0], local_sem.at[1]),
        pltpu.make_async_copy(v_hbm, space_buf.at[here, 1], local_sem.at[2]),
        pltpu.make_async_copy(mask_hbm, mask_ref, local_sem.at[3]),
        pltpu.make_async_copy(flags_hbm, flags_ref, local_sem.at[4]),
    ]

    barrier = pltpu.get_barrier_semaphore()
    expected = jnp.int32(0)
    for _, target, exists in routes:
        expected = expected + jnp.where(exists, 1, 0)

        @pl.when(exists)
        def _(target=target):
            pl.semaphore_signal(barrier, inc=1, device_id={"frame": target}, device_id_type=MESH)

    for other, near in partners:
        expected = expected + jnp.where(near, 1, 0)

        @pl.when(near)
        def _(other=other):
            pl.semaphore_signal(barrier, inc=1, device_id={"space": other}, device_id_type=MESH)

    for copy in local:
        copy.start()
    pl.semaphore_wait(barrier, expected)

    def frame_copy(way, hop, chunk, part, target):
        span = pl.ds(chunk * chunk_rows, chunk_rows)
        if hop == 1:
            source = (k_hbm, v_hbm)[part].at[span]
        else:
            source = frame_buf.at[way, hop - 2, part, span]
        return pltpu.make_async_remote_copy(
            src_ref=source,
            dst_ref=frame_buf.at[way, hop - 1, part, span],
            send_sem=frame_send.at[way, hop - 1, chunk, part],
            recv_sem=frame_recv.at[way, hop - 1, chunk, part],
            device_id={"frame": target},
            device_id_type=MESH,
        )

    def space_copy(step, part, slot, target):
        return pltpu.make_async_remote_copy(
            src_ref=(k_hbm, v_hbm)[part],
            dst_ref=space_buf.at[slot, part],
            send_sem=space_send.at[step, part],
            recv_sem=space_recv.at[slot, part],
            device_id={"space": target},
            device_id_type=MESH,
        )

    for chunk in range(chunks):
        for way, target, exists in routes:

            @pl.when(exists)
            def _(way=way, target=target, chunk=chunk):
                for part in range(2):
                    frame_copy(way, 1, chunk, part, target).start()

    for step, (other, near) in enumerate(partners):

        @pl.when(near)
        def _(step=step, other=other):
            for part in range(2):
                space_copy(step, part, here, other).start()

    for copy in local:
        copy.wait()

    scale = math.log2(math.e) / math.sqrt(width)
    first, second, third = pieces_of(q_vmem[...] * scale, 3)
    query_parts[...] = jnp.concatenate([first, second, second, first, third, first], axis=1)
    row_max[...] = jnp.full_like(row_max, masked_score)
    row_total[...] = jnp.zeros_like(row_total)
    weighted[...] = jnp.zeros_like(weighted)

    def absorb(key_rows, read_values, shift):
        k0, k1, k2 = pieces_of(key_rows, 3)
        scores = lax.dot_general(
            jnp.concatenate([k0, k1, k0, k1, k0, k2], axis=1),
            query_parts[...],
            (((1,), (1,)), ((), ())),
            preferred_element_type=jnp.float32,
        )
        old_max = row_max[...]
        new_max = jnp.maximum(old_max, jnp.max(scores, axis=0, keepdims=True) + shift)
        weights = jnp.exp2(scores - (new_max - shift))
        factor = jnp.exp2(old_max - new_max)
        row_max[...] = new_max
        row_total[...] = row_total[...] * factor + jnp.sum(weights, axis=0, keepdims=True)
        v_parts = jnp.concatenate(pieces_of(read_values(), 2), axis=1)
        w0, w1 = pieces_of(weights, 2)
        contract = (((0,), (0,)), ((), ()))
        product = lax.dot_general(v_parts, w0, contract, preferred_element_type=jnp.float32)
        product += lax.dot_general(v_parts, w1, contract, preferred_element_type=jnp.float32)
        weighted[...] = weighted[...] * factor + (product[:width] + product[width:])

    def absorb_space(slot, allowed):
        absorb(space_buf[slot, 0], lambda: space_buf[slot, 1], jnp.where(allowed > 0, 0.0, masked_score))

    def take_space(step):
        other, near = partners[step]

        @pl.when(near)
        def _():
            for part in range(2):
                space_copy(step, part, other, other).wait_recv()
            absorb_space(other, mask_ref[here, other])

    def arrives(way, hop):
        return (group >= hop) if way == 0 else (group + hop < groups)

    def take_frame(hop):
        used = hop & (hop - 1) == 0
        passed_on = hop < depth
        lag = min(2, chunks - 1) if hop == 1 else 0

        def pass_on(chunk):
            for way, target, exists in routes:

                @pl.when(arrives(way, hop) & exists)
                def _(way=way, target=target):
                    for part in range(2):
                        frame_copy(way, hop + 1, chunk, part, target).start()

        def attend(way, chunk, before_values):
            allowed = flags_ref[hop.bit_length() - 1, way, group]
            span = pl.ds(chunk * chunk_rows, chunk_rows)

            def read_values():
                before_values()
                return frame_buf[way, hop - 1, 1, span]

            absorb(
                frame_buf[way, hop - 1, 0, span],
                read_values,
                jnp.where(allowed > 0, 0.0, masked_score),
            )

        for chunk in range(chunks):
            for way, target, _ in routes:
                landed = [frame_copy(way, hop, chunk, part, target) for part in range(2)]
                if used and not passed_on:

                    @pl.when(arrives(way, hop))
                    def _(way=way, landed=landed):
                        landed[0].wait_recv()
                        attend(way, chunk, landed[1].wait_recv)

                else:

                    @pl.when(arrives(way, hop))
                    def _(landed=landed):
                        for copy in landed:
                            copy.wait_recv()

            if passed_on and chunk >= lag:
                pass_on(chunk - lag)
                if chunk == chunks - 1:
                    for late in range(chunks - lag, chunks):
                        pass_on(late)
            if used and passed_on:
                for way, _, _ in routes:

                    @pl.when(arrives(way, hop))
                    def _(way=way):
                        attend(way, chunk, lambda: None)

    absorb_space(here, mask_ref[here, here])
    take_space(0)
    take_frame(1)
    for step in range(1, blocks - 1):
        take_space(step)
    for hop in range(2, depth + 1):
        take_frame(hop)

    out_ref[...] = (weighted[...] / row_total[...]).T

    for step, (other, near) in enumerate(partners):

        @pl.when(near)
        def _(step=step, other=other):
            for part in range(2):
                space_copy(step, part, here, other).wait_send()

    for hop in range(1, depth + 1):
        for way, target, exists in routes:

            @pl.when(exists & arrives(way, hop - 1))
            def _(way=way, hop=hop, target=target):
                for chunk in range(chunks):
                    for part in range(2):
                        frame_copy(way, hop, chunk, part, target).wait_send()


def per_device(queries, keys, values, block_mask, partner_flags):
    rows, width = queries.shape
    blocks = lax.axis_size("space")
    groups = lax.axis_size("frame")
    levels = partner_flags.shape[1]
    depth = 2 ** (levels - 1)
    chunks = 4
    used = blocks + 2 * levels
    return pl.pallas_call(
        functools.partial(kernel, blocks, groups, levels, chunks),
        out_shape=jax.ShapeDtypeStruct((rows, width), jnp.float32),
        in_specs=[pl.BlockSpec(memory_space=pltpu.HBM)] * 5,
        out_specs=pl.BlockSpec(memory_space=pltpu.VMEM),
        scratch_shapes=[
            pltpu.SMEM(block_mask.shape, jnp.int32),
            pltpu.SMEM((levels, 2, groups), jnp.int32),
            pltpu.VMEM((rows, width), jnp.float32),
            pltpu.VMEM((blocks, 2, rows, width), jnp.float32),
            pltpu.VMEM((2, depth, 2, rows, width), jnp.float32),
            pltpu.VMEM((rows, 6 * width), jnp.bfloat16),
            pltpu.VMEM((1, rows), jnp.float32),
            pltpu.VMEM((1, rows), jnp.float32),
            pltpu.VMEM((width, rows), jnp.float32),
            pltpu.SemaphoreType.DMA((5,)),
            pltpu.SemaphoreType.DMA((blocks, 2)),
            pltpu.SemaphoreType.DMA((blocks, 2)),
            pltpu.SemaphoreType.DMA((2, depth, chunks, 2)),
            pltpu.SemaphoreType.DMA((2, depth, chunks, 2)),
        ],
        compiler_params=pltpu.CompilerParams(
            collective_id=0, has_side_effects=True, vmem_limit_bytes=60 * 2**20
        ),
        cost_estimate=pl.CostEstimate(
            flops=4 * used * rows * rows * width,
            bytes_accessed=16 * rows * width,
            transcendentals=used * rows * rows,
        ),
    )(queries, keys, values, block_mask, jnp.transpose(partner_flags, (1, 2, 0)))


def solution(mesh):
    split = P(("groups", "frame", "space"), None)
    return jax.shard_map(
        per_device,
        mesh=mesh,
        in_specs=(split, split, split, P(), P()),
        out_specs=split,
        check_vma=False,
    )
```

```python
import functools
import math

import jax
import jax.numpy as jnp
from jax import lax
from jax.experimental import pallas as pl
from jax.experimental.pallas import tpu as pltpu
from jax.sharding import PartitionSpec as P

masked_score = -1e30
MESH = pl.DeviceIdType.MESH


def pieces_of(block, count):
    pieces = []
    rest = block
    for index in range(count):
        piece = rest.astype(jnp.bfloat16)
        pieces.append(piece)
        if index + 1 < count:
            rest = rest - piece.astype(jnp.float32)
    return pieces


def kernel(
    blocks,
    groups,
    levels,
    chunks,
    q_hbm,
    k_hbm,
    v_hbm,
    mask_hbm,
    flags_hbm,
    out_ref,
    mask_ref,
    flags_ref,
    q_vmem,
    space_buf,
    frame_buf,
    query_parts,
    row_max,
    row_total,
    weighted,
    local_sem,
    space_send,
    space_recv,
    frame_send,
    frame_recv,
):
    rows, width = q_vmem.shape
    chunk_rows = rows // chunks
    depth = 2 ** (levels - 1)
    reach = blocks // 2
    chips = blocks // 2
    here = lax.axis_index("space")
    group = lax.axis_index("frame")

    partners = []
    for step in range(1, blocks):
        chip = lax.rem(here // 2 + step // 2, chips)
        core = lax.rem(here % 2 + step % 2, 2)
        other = chip * 2 + core
        distance = jnp.where(other > here, other - here, here - other)
        partners.append((other, distance <= reach))
    routes = [
        (0, group + 1, group + 1 < groups),
        (1, group - 1, group >= 1),
    ]

    local = [
        pltpu.make_async_copy(q_hbm, q_vmem, local_sem.at[0]),
        pltpu.make_async_copy(k_hbm, space_buf.at[here, 0], local_sem.at[1]),
        pltpu.make_async_copy(v_hbm, space_buf.at[here, 1], local_sem.at[2]),
        pltpu.make_async_copy(mask_hbm, mask_ref, local_sem.at[3]),
        pltpu.make_async_copy(flags_hbm, flags_ref, local_sem.at[4]),
    ]

    barrier = pltpu.get_barrier_semaphore()
    expected = jnp.int32(0)
    for _, target, exists in routes:
        expected = expected + jnp.where(exists, 1, 0)

        @pl.when(exists)
        def _(target=target):
            pl.semaphore_signal(barrier, inc=1, device_id={"frame": target}, device_id_type=MESH)

    for other, near in partners:
        expected = expected + jnp.where(near, 1, 0)

        @pl.when(near)
        def _(other=other):
            pl.semaphore_signal(barrier, inc=1, device_id={"space": other}, device_id_type=MESH)

    for copy in local:
        copy.start()
    pl.semaphore_wait(barrier, expected)

    def frame_copy(way, hop, chunk, part, target):
        span = pl.ds(chunk * chunk_rows, chunk_rows)
        if hop == 1:
            source = (k_hbm, v_hbm)[part].at[span]
        else:
            source = frame_buf.at[way, hop - 2, part, span]
        return pltpu.make_async_remote_copy(
            src_ref=source,
            dst_ref=frame_buf.at[way, hop - 1, part, span],
            send_sem=frame_send.at[way, hop - 1, chunk, part],
            recv_sem=frame_recv.at[way, hop - 1, chunk, part],
            device_id={"frame": target},
            device_id_type=MESH,
        )

    def space_copy(step, part, slot, target):
        return pltpu.make_async_remote_copy(
            src_ref=(k_hbm, v_hbm)[part],
            dst_ref=space_buf.at[slot, part],
            send_sem=space_send.at[step, part],
            recv_sem=space_recv.at[slot, part],
            device_id={"space": target},
            device_id_type=MESH,
        )

    for chunk in range(chunks):
        for way, target, exists in routes:

            @pl.when(exists)
            def _(way=way, target=target, chunk=chunk):
                for part in range(2):
                    frame_copy(way, 1, chunk, part, target).start()

    for step, (other, near) in enumerate(partners):

        @pl.when(near)
        def _(step=step, other=other):
            for part in range(2):
                space_copy(step, part, here, other).start()

    for copy in local:
        copy.wait()

    scale = math.log2(math.e) / math.sqrt(width)
    first, second, third = pieces_of(q_vmem[...] * scale, 3)
    query_parts[...] = jnp.concatenate([first, second, second, first, third, first], axis=1)
    row_max[...] = jnp.full_like(row_max, masked_score)
    row_total[...] = jnp.zeros_like(row_total)
    weighted[...] = jnp.zeros_like(weighted)

    def absorb(key_rows, read_values, shift):
        k0, k1, k2 = pieces_of(key_rows, 3)
        scores = lax.dot_general(
            jnp.concatenate([k0, k1, k0, k1, k0, k2], axis=1),
            query_parts[...],
            (((1,), (1,)), ((), ())),
            preferred_element_type=jnp.float32,
        )
        old_max = row_max[...]
        new_max = jnp.maximum(old_max, jnp.max(scores, axis=0, keepdims=True) + shift)
        weights = jnp.exp2(scores - (new_max - shift))
        factor = jnp.exp2(old_max - new_max)
        row_max[...] = new_max
        row_total[...] = row_total[...] * factor + jnp.sum(weights, axis=0, keepdims=True)
        v_parts = jnp.concatenate(pieces_of(read_values(), 2), axis=1)
        w0, w1 = pieces_of(weights, 2)
        contract = (((0,), (0,)), ((), ()))
        product = lax.dot_general(v_parts, w0, contract, preferred_element_type=jnp.float32)
        product += lax.dot_general(v_parts, w1, contract, preferred_element_type=jnp.float32)
        weighted[...] = weighted[...] * factor + (product[:width] + product[width:])

    def absorb_space(slot, allowed):
        absorb(space_buf[slot, 0], lambda: space_buf[slot, 1], jnp.where(allowed > 0, 0.0, masked_score))

    def take_space(step):
        other, near = partners[step]

        @pl.when(near)
        def _():
            for part in range(2):
                space_copy(step, part, other, other).wait_recv()
            absorb_space(other, mask_ref[here, other])

    def arrives(way, hop):
        return (group >= hop) if way == 0 else (group + hop < groups)

    def take_frame(hop):
        used = hop & (hop - 1) == 0
        passed_on = hop < depth
        lag = min(2, chunks - 1) if hop == 1 else 0

        def pass_on(chunk):
            for way, target, exists in routes:

                @pl.when(arrives(way, hop) & exists)
                def _(way=way, target=target):
                    for part in range(2):
                        frame_copy(way, hop + 1, chunk, part, target).start()

        def attend(way, chunk, before_values):
            allowed = flags_ref[hop.bit_length() - 1, way, group]
            span = pl.ds(chunk * chunk_rows, chunk_rows)

            def read_values():
                before_values()
                return frame_buf[way, hop - 1, 1, span]

            absorb(
                frame_buf[way, hop - 1, 0, span],
                read_values,
                jnp.where(allowed > 0, 0.0, masked_score),
            )

        for chunk in range(chunks):
            for way, target, _ in routes:
                landed = [frame_copy(way, hop, chunk, part, target) for part in range(2)]
                if used and not passed_on:

                    @pl.when(arrives(way, hop))
                    def _(way=way, landed=landed):
                        landed[0].wait_recv()
                        attend(way, chunk, landed[1].wait_recv)

                else:

                    @pl.when(arrives(way, hop))
                    def _(landed=landed):
                        for copy in landed:
                            copy.wait_recv()

            if passed_on and chunk >= lag:
                pass_on(chunk - lag)
                if chunk == chunks - 1:
                    for late in range(chunks - lag, chunks):
                        pass_on(late)
            if used and passed_on:
                for way, _, _ in routes:

                    @pl.when(arrives(way, hop))
                    def _(way=way):
                        attend(way, chunk, lambda: None)

    absorb_space(here, mask_ref[here, here])
    take_space(0)
    take_frame(1)
    for step in range(1, blocks - 1):
        take_space(step)
    for hop in range(2, depth + 1):
        take_frame(hop)

    out_ref[...] = (weighted[...] / row_total[...]).T

    for step, (other, near) in enumerate(partners):

        @pl.when(near)
        def _(step=step, other=other):
            for part in range(2):
                space_copy(step, part, here, other).wait_send()

    for hop in range(1, depth + 1):
        for way, target, exists in routes:

            @pl.when(exists & arrives(way, hop - 1))
            def _(way=way, hop=hop, target=target):
                for chunk in range(chunks):
                    for part in range(2):
                        frame_copy(way, hop, chunk, part, target).wait_send()


def per_device(queries, keys, values, block_mask, partner_flags):
    rows, width = queries.shape
    blocks = lax.axis_size("space")
    groups = lax.axis_size("frame")
    levels = partner_flags.shape[1]
    depth = 2 ** (levels - 1)
    chunks = 4
    used = blocks + 2 * levels
    arguments = [
        pltpu.with_memory_space_constraint(argument, pltpu.HBM)
        for argument in (queries, keys, values, block_mask, jnp.transpose(partner_flags, (1, 2, 0)))
    ]
    return pl.pallas_call(
        functools.partial(kernel, blocks, groups, levels, chunks),
        out_shape=jax.ShapeDtypeStruct((rows, width), jnp.float32),
        in_specs=[pl.BlockSpec(memory_space=pltpu.HBM)] * 5,
        out_specs=pl.BlockSpec(memory_space=pltpu.VMEM),
        scratch_shapes=[
            pltpu.SMEM(block_mask.shape, jnp.int32),
            pltpu.SMEM((levels, 2, groups), jnp.int32),
            pltpu.VMEM((rows, width), jnp.float32),
            pltpu.VMEM((blocks, 2, rows, width), jnp.float32),
            pltpu.VMEM((2, depth, 2, rows, width), jnp.float32),
            pltpu.VMEM((rows, 6 * width), jnp.bfloat16),
            pltpu.VMEM((1, rows), jnp.float32),
            pltpu.VMEM((1, rows), jnp.float32),
            pltpu.VMEM((width, rows), jnp.float32),
            pltpu.SemaphoreType.DMA((5,)),
            pltpu.SemaphoreType.DMA((blocks, 2)),
            pltpu.SemaphoreType.DMA((blocks, 2)),
            pltpu.SemaphoreType.DMA((2, depth, chunks, 2)),
            pltpu.SemaphoreType.DMA((2, depth, chunks, 2)),
        ],
        compiler_params=pltpu.CompilerParams(
            collective_id=0, has_side_effects=True, vmem_limit_bytes=48 * 2**20
        ),
        cost_estimate=pl.CostEstimate(
            flops=4 * used * rows * rows * width,
            bytes_accessed=16 * rows * width,
            transcendentals=used * rows * rows,
        ),
    )(*arguments)


def solution(mesh):
    split = P(("groups", "frame", "space"), None)
    return jax.shard_map(
        per_device,
        mesh=mesh,
        in_specs=(split, split, split, P(), P()),
        out_specs=split,
        check_vma=False,
    )
```
